256 devices in a mesh: rows: 8 (over z_lo, x), cols: 32 (over y, z_hi, core).
Axes of the slice: x: 4, y: 4, z: 8 (z_hi: 4, z_lo: 2; z = z_hi * 2 + z_lo), core: 2. Of those that a mesh axis runs over, the one named last changes fastest.
Arguments:
- embeddings: float32 [1024, 16384], P('rows', 'cols'), may hold values from -70 to 70
Outputs:
- grad_scaled: float32 [1024, 16384], P('rows', 'cols')
- loss: float32 [], replicated
The draws below stay inside these ranges and needn't reach their ends.
All inputs are finite; a program needn't handle non-finite values.
Results may differ from the reference program's by a relative error of at most 0.0003.
The reference program's roundings to bfloat16 on the way (of `centered`) count: a program that leaves them out, or rounds other values in their place, can miss the bound.
Values may be sent and summed in bfloat16 or wider, within the bound.
No kernel may reach another device: no remote copies, remote signals or barrier semaphores. Data moves between devices by JAX's collectives and lax.ppermute only.
A program may use at most 64 MiB of HBM per device.

```python
import math
import jax
import jax.numpy as jnp
from jax import lax

WIDTH = 16384
N_ALL = 1024
N_COLS = 32


def draw_embeddings(key, part):
    key = jax.random.fold_in(key, 7)
    keys = jax.random.split(key, 4)
    position = jnp.arange(N_ALL, dtype=jnp.float32) / N_ALL
    rise = 0.5 + position
    row_scale = jnp.exp(jax.random.uniform(keys[0], (N_ALL,), jnp.float32, math.log(0.4), math.log(4.0)))
    col_scale = jnp.exp(jax.random.uniform(keys[1], (WIDTH,), jnp.float32, math.log(0.3), math.log(3.0)))
    offset = jax.random.uniform(keys[2], (WIDTH,), jnp.float32, -1.5, 1.5)
    noise = jnp.clip(jax.random.normal(keys[3], (N_ALL, WIDTH), jnp.float32), -4.0, 4.0)
    values = (offset[None, :] * rise[:, None] + noise * row_scale[:, None]) * col_scale[None, :]
    return values.astype(jnp.float32)


def setup_inputs(seed: int = 0) -> dict:
    splits = jax.random.split(jax.random.key(seed), 2)
    embeddings = draw_embeddings(jax.random.fold_in(splits[1], 71), 0)
    return dict(embeddings=embeddings)


def reference(embeddings):
    n_all = embeddings.shape[0]
    width = embeddings.shape[1]
    col_width = width // N_COLS
    mean = lax.optimization_barrier(jnp.sum(embeddings, axis=0)) / n_all
    cz = embeddings - mean
    var = lax.optimization_barrier(jnp.sum(cz * cz, axis=0)) / (n_all - 1)
    std = jnp.sqrt(var + 0.0001)
    var_loss = jnp.mean(jax.nn.relu(1.0 - std))
    centered = cz.astype(jnp.bfloat16)
    wide_f32 = centered.astype(jnp.float32)

    def one_block(block_index):
        first = (block_index * col_width).astype(jnp.int32)
        local_cols = lax.dynamic_slice_in_dim(wide_f32, first, col_width, 1)
        cov = jnp.dot(local_cols.T, wide_f32, precision=lax.Precision.HIGHEST) / (n_all - 1)
        row_ids = first + lax.broadcasted_iota(jnp.int32, (col_width, width), 0)
        col_ids = lax.broadcasted_iota(jnp.int32, (col_width, width), 1)
        offdiag = jnp.where(row_ids == col_ids, jnp.float32(0.0), cov)
        loss_part = jnp.sum(offdiag * offdiag)
        grad_cols = jnp.dot(wide_f32, offdiag.T, precision=lax.Precision.HIGHEST)
        return (grad_cols, loss_part)
    grads, parts = lax.map(one_block, jnp.arange(N_COLS))
    grad_cov = jnp.transpose(grads, (1, 0, 2)).reshape(n_all, width)
    cov_loss = jnp.sum(parts) / width
    loss = 25.0 * var_loss + cov_loss
    hinge = jnp.where(std < 1.0, cz / std, jnp.float32(0.0))
    grad_scaled = 4.0 / 25.0 * grad_cov - hinge
    return (grad_scaled, loss)
```

```python
import jax
import jax.numpy as jnp
from jax import lax
from jax.sharding import Mesh
from jax.sharding import PartitionSpec as P

ROWS = ("zl", "x")
CHIPS = ("y", "zh")
SWAP = [(0, 1), (1, 0)]
F32 = jnp.float32
BF16 = jnp.bfloat16


def spread(block, axes, count):
    return lax.all_to_all(jnp.broadcast_to(block, (count,) + block.shape), axes, 0, 0)


def three_terms(a):
    high = lax.reduce_precision(a, 8, 7)
    rest = a - high
    mid = lax.reduce_precision(rest, 8, 7)
    low = rest - mid
    return jnp.concatenate([high.astype(BF16), mid.astype(BF16), low.astype(BF16)], axis=0)


def on_device(embeddings):
    rows_here, col_width = embeddings.shape
    rows_count = lax.axis_size(ROWS)
    chips_count = lax.axis_size(CHIPS)
    cols_count = chips_count * lax.axis_size("core")
    core = lax.axis_index("core")
    n_all = rows_here * rows_count
    width = col_width * cols_count
    scale = F32(n_all - 1)

    sum_here = jnp.sum(embeddings, axis=0)
    off_here = embeddings - sum_here / rows_here
    squares_here = jnp.sum(off_here * off_here, axis=0)
    stats = spread(jnp.stack([sum_here, squares_here]), ROWS, rows_count)
    sums, squares = stats[:, 0], stats[:, 1]
    mean = jnp.sum(sums, axis=0) / n_all
    gaps = sums / rows_here - mean
    var = (jnp.sum(squares, axis=0) + rows_here * jnp.sum(gaps * gaps, axis=0)) / scale
    std = jnp.sqrt(var + 0.0001)

    cz = embeddings - mean
    centered = cz.astype(BF16)
    gathered = spread(centered, ROWS, rows_count).reshape(n_all, col_width)

    gathered_f32 = gathered.astype(F32)
    col_norms = jnp.sum(gathered_f32 * gathered_f32, axis=0)
    block_share = (
        25.0 * jnp.sum(jax.nn.relu(1.0 - std)) - jnp.sum(col_norms * col_norms) / (scale * scale)
    ) / width

    half = rows_here // 2

    def half_gram(which):
        own = lax.dynamic_slice_in_dim(centered, which * half, half, 0)
        gram = lax.dot_general(
            own, gathered, (((1,), (1,)), ((), ())), preferred_element_type=F32
        )
        return jnp.concatenate([gram, jnp.full((half, 128), block_share)], axis=1)

    from_pair = lax.ppermute(half_gram(1 - core), "core", SWAP)
    chip_half = half_gram(core) + from_pair
    piece = half // chips_count
    pieces = lax.all_to_all(chip_half.reshape(chips_count, piece, n_all + 128), CHIPS, 0, 0)
    mine = jnp.sum(pieces, axis=0)
    blocks_share = mine[0, n_all]
    my_half = spread(mine[:, :n_all], CHIPS, chips_count).reshape(half, n_all)

    norm = jnp.sum(my_half * my_half)
    for axis, perm in (
        ("core", SWAP),
        ("zl", SWAP),
        ("x", [(0, 1), (1, 0), (2, 3), (3, 2)]),
        ("x", [(0, 2), (2, 0), (1, 3), (3, 1)]),
    ):
        norm = norm + lax.ppermute(norm, axis, perm)
    loss = norm / (scale * scale * width) + blocks_share

    other_half = lax.ppermute(my_half, "core", SWAP)
    first = jnp.where(core == 0, my_half, other_half)
    second = jnp.where(core == 0, other_half, my_half)
    gram = jnp.concatenate([first, second], axis=0)
    terms = jnp.dot(three_terms(gram), gathered, preferred_element_type=F32)
    product = terms[:rows_here] + terms[rows_here : 2 * rows_here] + terms[2 * rows_here :]
    grad_cov = (product - centered.astype(F32) * col_norms) / scale
    hinge = jnp.where(std < 1.0, cz / std, F32(0.0))
    return (4.0 / 25.0 * grad_cov - hinge, loss)


def solution(mesh):
    parts = Mesh(mesh.devices.reshape(2, 4, 4, 4, 2), ("zl", "x", "y", "zh", "core"))
    placed = P(("zl", "x"), ("y", "zh", "core"))
    return jax.shard_map(
        on_device, mesh=parts, in_specs=(placed,), out_specs=(placed, P()), check_vma=False
    )
```

```python
import jax
import jax.numpy as jnp
from jax import lax
from jax.sharding import Mesh
from jax.sharding import PartitionSpec as P

ROWS = ("zl", "x")
SWAP = [(0, 1), (1, 0)]
F32 = jnp.float32
BF16 = jnp.bfloat16


def spread(block, axes, count):
    return lax.all_to_all(jnp.broadcast_to(block, (count,) + block.shape), axes, 0, 0)


def shift(block, axis, k):
    size = lax.axis_size(axis)
    return lax.ppermute(block, axis, [(i, (i + k) % size) for i in range(size)])


def three_terms(a):
    high = lax.reduce_precision(a, 8, 7)
    rest = a - high
    mid = lax.reduce_precision(rest, 8, 7)
    low = rest - mid
    return jnp.concatenate([high.astype(BF16), mid.astype(BF16), low.astype(BF16)], axis=0)


def on_device(embeddings):
    rows_here, col_width = embeddings.shape
    rows_count = lax.axis_size(ROWS)
    ys = lax.axis_size("y")
    cols_count = ys * lax.axis_size("zh") * lax.axis_size("core")
    core = lax.axis_index("core")
    y = lax.axis_index("y")
    n_all = rows_here * rows_count
    width = col_width * cols_count
    scale = F32(n_all - 1)

    sum_here = jnp.sum(embeddings, axis=0)
    off_here = embeddings - sum_here / rows_here
    squares_here = jnp.sum(off_here * off_here, axis=0)
    stats = spread(jnp.stack([sum_here, squares_here]), ROWS, rows_count)
    sums, squares = stats[:, 0], stats[:, 1]
    mean = jnp.sum(sums, axis=0) / n_all
    gaps = sums / rows_here - mean
    var = (jnp.sum(squares, axis=0) + rows_here * jnp.sum(gaps * gaps, axis=0)) / scale
    std = jnp.sqrt(var + 0.0001)

    cz = embeddings - mean
    centered = cz.astype(BF16)
    gathered = spread(centered, ROWS, rows_count).reshape(n_all, col_width)

    gathered_f32 = gathered.astype(F32)
    col_norms = jnp.sum(gathered_f32 * gathered_f32, axis=0)
    block_share = (
        25.0 * jnp.sum(jax.nn.relu(1.0 - std)) - jnp.sum(col_norms * col_norms) / (scale * scale)
    ) / width

    half = rows_here // 2
    piece = half // ys

    def half_gram(which):
        own = lax.dynamic_slice_in_dim(centered, which * half, half, 0)
        own = lax.dynamic_slice_in_dim(jnp.concatenate([own, own]), y * piece, half, 0)
        gram = lax.dot_general(
            own, gathered, (((1,), (1,)), ((), ())), preferred_element_type=F32
        )
        return jnp.concatenate([gram, jnp.full((half, 128), block_share)], axis=1)

    from_pair = lax.ppermute(half_gram(1 - core), "core", SWAP)
    chip_half = half_gram(core) + from_pair
    chunks = [chip_half[k * piece : (k + 1) * piece] for k in range(ys)]
    over_y = chunks[0] + sum(shift(chunks[k], "y", k) for k in (2, 1, 3))
    mine = over_y + sum(shift(over_y, "zh", k) for k in (2, 1, 3))
    blocks_share = mine[0, n_all]
    mine = mine[:, :n_all]
    back = {k: shift(mine, "y", k) for k in (2, 1, 3)}
    around = jnp.concatenate([back[3], back[2], back[1], mine] * 2)
    my_half = lax.dynamic_slice_in_dim(around, (ys - 1 - y) * piece, half, 0)
    other_half = lax.ppermute(my_half, "core", SWAP)

    norm_here = jnp.sum(my_half * my_half)
    norms = spread(jnp.full((128,), norm_here), ROWS + ("core",), 2 * rows_count)
    norm = jnp.sum(norms[:, 0])
    loss = norm / (scale * scale * width) + blocks_share

    first = jnp.where(core == 0, my_half, other_half)
    second = jnp.where(core == 0, other_half, my_half)
    gram = jnp.concatenate([first, second], axis=0)
    terms = jnp.dot(three_terms(gram), gathered, preferred_element_type=F32)
    product = terms[:rows_here] + terms[rows_here : 2 * rows_here] + terms[2 * rows_here :]
    grad_cov = (product - centered.astype(F32) * col_norms) / scale
    hinge = jnp.where(std < 1.0, cz / std, F32(0.0))
    return (4.0 / 25.0 * grad_cov - hinge, loss)


def solution(mesh):
    parts = Mesh(mesh.devices.reshape(2, 4, 4, 4, 2), ("zl", "x", "y", "zh", "core"))
    placed = P(("zl", "x"), ("y", "zh", "core"))
    return jax.shard_map(
        on_device, mesh=parts, in_specs=(placed,), out_specs=(placed, P()), check_vma=False
    )
```

```python
import jax
import jax.numpy as jnp
from jax import lax
from jax.sharding import Mesh
from jax.sharding import PartitionSpec as P

ROWS = ("zl", "x")
SWAP = [(0, 1), (1, 0)]
F32 = jnp.float32
BF16 = jnp.bfloat16


def spread(block, axes, count):
    return lax.all_to_all(jnp.broadcast_to(block, (count,) + block.shape), axes, 0, 0)


def shift(block, axis, k):
    size = lax.axis_size(axis)
    return lax.ppermute(block, axis, [(i, (i + k) % size) for i in range(size)])


def three_terms(a):
    high = lax.reduce_precision(a, 8, 7)
    rest = a - high
    mid = lax.reduce_precision(rest, 8, 7)
    low = rest - mid
    return jnp.concatenate([high.astype(BF16), mid.astype(BF16), low.astype(BF16)], axis=0)


def lanes(a):
    return jnp.sum(a.reshape(-1, 128), axis=0)


def on_device(embeddings):
    rows_here, col_width = embeddings.shape
    rows_count = lax.axis_size(ROWS)
    ys = lax.axis_size("y")
    cols_count = ys * lax.axis_size("zh") * lax.axis_size("core")
    core = lax.axis_index("core")
    y = lax.axis_index("y")
    n_all = rows_here * rows_count
    width = col_width * cols_count
    scale = F32(n_all - 1)

    sum_here = jnp.sum(embeddings, axis=0)
    off_here = embeddings - sum_here / rows_here
    squares_here = jnp.sum(off_here * off_here, axis=0)
    stats = spread(jnp.stack([sum_here, squares_here]), ROWS, rows_count)
    sums, squares = stats[:, 0], stats[:, 1]
    mean = jnp.sum(sums, axis=0) / n_all
    gaps = sums / rows_here - mean
    var = (jnp.sum(squares, axis=0) + rows_here * jnp.sum(gaps * gaps, axis=0)) / scale
    std = jnp.sqrt(var + 0.0001)

    cz = embeddings - mean
    centered = cz.astype(BF16)
    gathered = spread(centered, ROWS, rows_count).reshape(n_all, col_width)

    half = rows_here // 2
    piece = half // ys

    def half_gram(which):
        own = lax.dynamic_slice_in_dim(centered, which * half, half, 0)
        own = lax.dynamic_slice_in_dim(jnp.concatenate([own, own]), y * piece, half, 0)
        return lax.dot_general(
            own, gathered, (((1,), (1,)), ((), ())), preferred_element_type=F32
        )

    from_pair = lax.ppermute(half_gram(1 - core), "core", SWAP)
    chip_half = half_gram(core) + from_pair
    chunks = [chip_half[k * piece : (k + 1) * piece] for k in range(ys)]
    over_y = chunks[0] + sum(shift(chunks[k], "y", k) for k in (2, 1, 3))

    gathered_f32 = gathered.astype(F32)
    col_norms = jnp.sum(gathered_f32 * gathered_f32, axis=0)
    block_share = (
        25.0 * lanes(jax.nn.relu(1.0 - std)) - lanes(col_norms * col_norms) / (scale * scale)
    ) / (width * rows_count)
    over_y = jnp.concatenate([over_y, jnp.broadcast_to(block_share, (piece, 128))], axis=1)
    mine = over_y + sum(shift(over_y, "zh", k) for k in (2, 1, 3))
    blocks = [mine] + [shift(mine, "y", k) for k in (1, 2, 3)]
    my_half = jnp.concatenate([block[:, :n_all] for block in blocks])
    other_half = lax.ppermute(my_half, "core", SWAP)
    blocks_share = sum(block[0, n_all:] for block in blocks)
    share = lanes(my_half * my_half) / (scale * scale * width) + blocks_share
    shares = spread(share, ROWS + ("core",), rows_count * 2)

    gram = jnp.zeros((rows_here, n_all), F32)
    for k in range(ys):
        owner = lax.rem(y + ys - k, ys)
        for c, rows in enumerate((my_half, other_half)):
            block = rows[k * piece : (k + 1) * piece]
            start = lax.rem(core + c, 2) * half + owner * piece
            gram = lax.dynamic_update_slice_in_dim(gram, block, start, 0)
    terms = jnp.dot(three_terms(gram), gathered, preferred_element_type=F32)
    product = terms[:rows_here] + terms[rows_here : 2 * rows_here] + terms[2 * rows_here :]
    grad_cov = (product - centered.astype(F32) * col_norms) / scale
    hinge = jnp.where(std < 1.0, cz / std, F32(0.0))
    grad_scaled = 4.0 / 25.0 * grad_cov - hinge
    grad_scaled, shares = lax.optimization_barrier((grad_scaled, shares))
    return (grad_scaled, jnp.sum(shares))


def solution(mesh):
    parts = Mesh(mesh.devices.reshape(2, 4, 4, 4, 2), ("zl", "x", "y", "zh", "core"))
    placed = P(("zl", "x"), ("y", "zh", "core"))
    return jax.shard_map(
        on_device, mesh=parts, in_specs=(placed,), out_specs=(placed, P()), check_vma=False
    )
```

```python
import jax
import jax.numpy as jnp
from jax import lax
from jax.experimental import pallas as pl
from jax.experimental.pallas import tpu as pltpu
from jax.sharding import Mesh
from jax.sharding import PartitionSpec as P

ROWS = ("zl", "x")
SWAP = [(0, 1), (1, 0)]
F32 = jnp.float32
BF16 = jnp.bfloat16


def spread(block, axes, count):
    return lax.all_to_all(jnp.broadcast_to(block, (count,) + block.shape), axes, 0, 0)


def shift(block, axis, k):
    size = lax.axis_size(axis)
    return lax.ppermute(block, axis, [(i, (i + k) % size) for i in range(size)])


RAW_MOVES = ((1, 0), (0, 1), (0, 3))


def move(block, along_zl, along_x):
    zls, xs = lax.axis_size("zl"), lax.axis_size("x")
    return lax.ppermute(
        block,
        ROWS,
        [
            (z * xs + x, (z + along_zl) % zls * xs + (x + along_x) % xs)
            for z in range(zls)
            for x in range(xs)
        ],
    )


def stats_kernel(block_ref, out_ref):
    block = block_ref[...]
    total = jnp.sum(block, axis=0, keepdims=True)
    off = block - total / block.shape[0]
    squares = jnp.sum(off * off, axis=0, keepdims=True)
    both = jnp.concatenate([total, squares], axis=0)
    for k in range(out_ref.shape[0]):
        out_ref[k] = both


def whole(count):
    return [pl.BlockSpec(memory_space=pltpu.VMEM)] * count


def three_terms(a):
    high = lax.reduce_precision(a, 8, 7)
    rest = a - high
    mid = lax.reduce_precision(rest, 8, 7)
    low = rest - mid
    return jnp.concatenate([high.astype(BF16), mid.astype(BF16), low.astype(BF16)], axis=0)


def lanes(a):
    return jnp.sum(a.reshape(-1, 128), axis=0)


def on_device(embeddings):
    rows_here, col_width = embeddings.shape
    rows_count = lax.axis_size(ROWS)
    ys = lax.axis_size("y")
    cols_count = ys * lax.axis_size("zh") * lax.axis_size("core")
    core = lax.axis_index("core")
    y = lax.axis_index("y")
    n_all = rows_here * rows_count
    width = col_width * cols_count
    scale = F32(n_all - 1)

    raw = [move(embeddings, *by) for by in RAW_MOVES]

    stats_here = pl.pallas_call(
        stats_kernel,
        out_shape=jax.ShapeDtypeStruct((rows_count, 2, col_width), F32),
        in_specs=whole(1),
        out_specs=whole(1)[0],
        name="stats",
    )(embeddings)
    stats = lax.all_to_all(stats_here, ROWS, 0, 0)
    stats, raw = lax.optimization_barrier((stats, raw))
    sums, squares = stats[:, 0], stats[:, 1]
    mean = jnp.sum(sums, axis=0) / n_all
    gaps = sums / rows_here - mean
    var = (jnp.sum(squares, axis=0) + rows_here * jnp.sum(gaps * gaps, axis=0)) / scale
    std = jnp.sqrt(var + 0.0001)

    cz = embeddings - mean
    centered = cz.astype(BF16)
    along_zl, along_x = (
        jnp.concatenate([(block - mean).astype(BF16) for block in pair])
        for pair in ((embeddings, raw[0]), raw[1:])
    )
    gathered = jnp.concatenate([along_zl, along_x, move(along_zl, 0, 2), move(along_x, 1, 0)])

    half = rows_here // 2
    piece = half // ys

    def half_gram(which):
        own = lax.dynamic_slice_in_dim(centered, which * half, half, 0)
        own = lax.dynamic_slice_in_dim(jnp.concatenate([own, own]), y * piece, half, 0)
        return lax.dot_general(
            own, gathered, (((1,), (1,)), ((), ())), preferred_element_type=F32
        )

    from_pair = lax.ppermute(half_gram(1 - core), "core", SWAP)
    chip_half = half_gram(core) + from_pair
    chunks = [chip_half[k * piece : (k + 1) * piece] for k in range(ys)]
    over_y = chunks[0] + sum(shift(chunks[k], "y", k) for k in (2, 1, 3))

    gathered_f32 = gathered.astype(F32)
    col_norms = jnp.sum(gathered_f32 * gathered_f32, axis=0)
    block_share = (
        25.0 * lanes(jax.nn.relu(1.0 - std)) - lanes(col_norms * col_norms) / (scale * scale)
    ) / (width * rows_count)
    over_y = jnp.concatenate([over_y, jnp.broadcast_to(block_share, (piece, 128))], axis=1)
    mine = over_y + sum(shift(over_y, "zh", k) for k in (2, 1, 3))
    blocks = [mine] + [shift(mine, "y", k) for k in (1, 2, 3)]
    my_half = jnp.concatenate([block[:, :n_all] for block in blocks])
    other_half = lax.ppermute(my_half, "core", SWAP)
    blocks_share = sum(block[0, n_all:] for block in blocks)
    share = lanes(my_half * my_half) / (scale * scale * width) + blocks_share
    shares = spread(jnp.broadcast_to(share, (8, 128)), ROWS + ("core",), rows_count * 2)

    gram = jnp.zeros((rows_here, n_all), F32)
    for k in range(ys):
        owner = lax.rem(y + ys - k, ys)
        for c, rows in enumerate((my_half, other_half)):
            block = rows[k * piece : (k + 1) * piece]
            start = lax.rem(core + c, 2) * half + owner * piece
            gram = lax.dynamic_update_slice_in_dim(gram, block, start, 0)
    terms = jnp.dot(three_terms(gram), gathered, preferred_element_type=F32)
    product = terms[:rows_here] + terms[rows_here : 2 * rows_here] + terms[2 * rows_here :]
    grad_cov = (product - centered.astype(F32) * col_norms) / scale
    hinge = jnp.where(std < 1.0, cz / std, F32(0.0))
    grad_scaled = 4.0 / 25.0 * grad_cov - hinge
    grad_scaled, shares = lax.optimization_barrier((grad_scaled, shares))
    return (grad_scaled, jnp.sum(shares[:, 0]))


def solution(mesh):
    parts = Mesh(mesh.devices.reshape(2, 4, 4, 4, 2), ("zl", "x", "y", "zh", "core"))
    placed = P(("zl", "x"), ("y", "zh", "core"))
    return jax.shard_map(
        on_device, mesh=parts, in_specs=(placed,), out_specs=(placed, P()), check_vma=False
    )
```

```python
import jax
import jax.numpy as jnp
from jax import lax
from jax.experimental import pallas as pl
from jax.experimental.pallas import tpu as pltpu
from jax.sharding import Mesh
from jax.sharding import PartitionSpec as P

ROWS = ("zl", "x")
SWAP = [(0, 1), (1, 0)]
F32 = jnp.float32
BF16 = jnp.bfloat16


def spread(block, axes, count):
    return lax.all_to_all(jnp.broadcast_to(block, (count,) + block.shape), axes, 0, 0)


def shift(block, axis, k):
    size = lax.axis_size(axis)
    return lax.ppermute(block, axis, [(i, (i + k) % size) for i in range(size)])


RAW_MOVES = ((1, 0), (0, 1), (0, 3))


def move(block, along_zl, along_x):
    zls, xs = lax.axis_size("zl"), lax.axis_size("x")
    return lax.ppermute(
        block,
        ROWS,
        [
            (z * xs + x, (z + along_zl) % zls * xs + (x + along_x) % xs)
            for z in range(zls)
            for x in range(xs)
        ],
    )


def stats_kernel(block_ref, out_ref):
    block = block_ref[...]
    total = jnp.sum(block, axis=0, keepdims=True)
    off = block - total / block.shape[0]
    squares = jnp.sum(off * off, axis=0, keepdims=True)
    both = jnp.concatenate([total, squares], axis=0)
    for k in range(out_ref.shape[0]):
        out_ref[k] = both


def whole(count):
    return [pl.BlockSpec(memory_space=pltpu.VMEM)] * count


def three_terms(a):
    high = lax.reduce_precision(a, 8, 7)
    rest = a - high
    mid = lax.reduce_precision(rest, 8, 7)
    low = rest - mid
    return jnp.concatenate([high.astype(BF16), mid.astype(BF16), low.astype(BF16)], axis=0)


def lanes(a):
    return jnp.sum(a.reshape(-1, 128), axis=0)


def on_device(embeddings):
    rows_here, col_width = embeddings.shape
    rows_count = lax.axis_size(ROWS)
    ys = lax.axis_size("y")
    cols_count = ys * lax.axis_size("zh") * lax.axis_size("core")
    core = lax.axis_index("core")
    y = lax.axis_index("y")
    n_all = rows_here * rows_count
    width = col_width * cols_count
    scale = F32(n_all - 1)

    raw = [move(embeddings, *by) for by in RAW_MOVES]

    stats_here = pl.pallas_call(
        stats_kernel,
        out_shape=jax.ShapeDtypeStruct((rows_count, 2, col_width), F32),
        in_specs=whole(1),
        out_specs=whole(1)[0],
        name="stats",
    )(embeddings)
    stats = lax.all_to_all(stats_here, ROWS, 0, 0)
    stats, raw, minus = lax.optimization_barrier((stats, raw, -embeddings))
    sums, squares = stats[:, 0], stats[:, 1]
    mean = jnp.sum(sums, axis=0) / n_all
    gaps = sums / rows_here - mean
    var = (jnp.sum(squares, axis=0) + rows_here * jnp.sum(gaps * gaps, axis=0)) / scale
    std = jnp.sqrt(var + 0.0001)

    cz = -(minus + mean)
    along_zl, along_x = (
        jnp.concatenate([block.astype(BF16) for block in pair])
        for pair in ((cz, raw[0] - mean), (raw[1] - mean, raw[2] - mean))
    )
    centered = along_zl[:rows_here]
    gathered = jnp.concatenate([along_zl, along_x, move(along_zl, 0, 2), move(along_x, 1, 0)])

    half = rows_here // 2
    piece = half // ys

    def half_gram(which):
        own = lax.dynamic_slice_in_dim(centered, which * half, half, 0)
        own = lax.dynamic_slice_in_dim(jnp.concatenate([own, own]), y * piece, half, 0)
        return lax.dot_general(
            own, gathered, (((1,), (1,)), ((), ())), preferred_element_type=F32
        )

    from_pair = lax.ppermute(half_gram(1 - core), "core", SWAP)
    from_pair, here = lax.optimization_barrier((from_pair, half_gram(core)))
    chip_half = here + from_pair
    chunks = [chip_half[k * piece : (k + 1) * piece] for k in range(ys)]
    over_y = chunks[0] + sum(shift(chunks[k], "y", k) for k in (2, 1, 3))

    gathered_f32 = gathered.astype(F32)
    col_norms = jnp.sum(gathered_f32 * gathered_f32, axis=0)
    block_share = (
        25.0 * lanes(jax.nn.relu(1.0 - std)) - lanes(col_norms * col_norms) / (scale * scale)
    ) / (width * rows_count)
    over_y = jnp.concatenate([over_y, jnp.broadcast_to(block_share, (piece, 128))], axis=1)
    mine = over_y + sum(shift(over_y, "zh", k) for k in (3, 2, 1))
    back = {k: shift(mine, "y", k) for k in (2, 1, 3)}
    blocks = [mine, back[1], back[2], back[3]]
    my_half = jnp.concatenate([block[:, :n_all] for block in blocks])
    other_half = lax.ppermute(my_half, "core", SWAP)
    blocks_share = sum(block[0, n_all:] for block in blocks)
    share = lanes(my_half * my_half) / (scale * scale * width) + blocks_share
    shares = spread(jnp.broadcast_to(share, (8, 128)), ROWS + ("core",), rows_count * 2)

    gram = jnp.zeros((rows_here, n_all), F32)
    for k in range(ys):
        owner = lax.rem(y + ys - k, ys)
        for c, rows in enumerate((my_half, other_half)):
            block = rows[k * piece : (k + 1) * piece]
            start = lax.rem(core + c, 2) * half + owner * piece
            gram = lax.dynamic_update_slice_in_dim(gram, block, start, 0)
    terms = jnp.dot(three_terms(gram), gathered, preferred_element_type=F32)
    product = terms[:rows_here] + terms[rows_here : 2 * rows_here] + terms[2 * rows_here :]
    grad_cov = (product - centered.astype(F32) * col_norms) / scale
    hinge = jnp.where(std < 1.0, cz / std, F32(0.0))
    grad_scaled = 4.0 / 25.0 * grad_cov - hinge
    grad_scaled, shares = lax.optimization_barrier((grad_scaled, shares))
    return (grad_scaled, jnp.sum(shares[:, 0]))


def solution(mesh):
    parts = Mesh(mesh.devices.reshape(2, 4, 4, 4, 2), ("zl", "x", "y", "zh", "core"))
    placed = P(("zl", "x"), ("y", "zh", "core"))
    return jax.shard_map(
        on_device, mesh=parts, in_specs=(placed,), out_specs=(placed, P()), check_vma=False
    )
```

```python
import jax
import jax.numpy as jnp
from jax import lax
from jax.experimental import pallas as pl
from jax.experimental.pallas import tpu as pltpu
from jax.sharding import Mesh
from jax.sharding import PartitionSpec as P

ROWS = ("zl", "x")
SWAP = [(0, 1), (1, 0)]
F32 = jnp.float32
BF16 = jnp.bfloat16


def spread(block, axes, count):
    return lax.all_to_all(jnp.broadcast_to(block, (count,) + block.shape), axes, 0, 0)


def shift(block, axis, k):
    size = lax.axis_size(axis)
    return lax.ppermute(block, axis, [(i, (i + k) % size) for i in range(size)])


RAW_MOVES = ((1, 0), (0, 1), (0, 3))


def move(block, along_zl, along_x):
    zls, xs = lax.axis_size("zl"), lax.axis_size("x")
    return lax.ppermute(
        block,
        ROWS,
        [
            (z * xs + x, (z + along_zl) % zls * xs + (x + along_x) % xs)
            for z in range(zls)
            for x in range(xs)
        ],
    )


def stats_kernel(block_ref, out_ref):
    block = block_ref[...]
    total = jnp.sum(block, axis=0, keepdims=True)
    off = block - total / block.shape[0]
    squares = jnp.sum(off * off, axis=0, keepdims=True)
    both = jnp.concatenate([total, squares], axis=0)
    for k in range(out_ref.shape[0]):
        out_ref[k] = both


def whole(count):
    return [pl.BlockSpec(memory_space=pltpu.VMEM)] * count


def three_terms(a):
    high = lax.reduce_precision(a, 8, 7)
    rest = a - high
    mid = lax.reduce_precision(rest, 8, 7)
    low = rest - mid
    return jnp.concatenate([high.astype(BF16), mid.astype(BF16), low.astype(BF16)], axis=0)


def lanes(a):
    return jnp.sum(a.reshape(-1, 128), axis=0)


def on_device(embeddings):
    rows_here, col_width = embeddings.shape
    rows_count = lax.axis_size(ROWS)
    ys = lax.axis_size("y")
    cols_count = ys * lax.axis_size("zh") * lax.axis_size("core")
    core = lax.axis_index("core")
    y = lax.axis_index("y")
    n_all = rows_here * rows_count
    width = col_width * cols_count
    scale = F32(n_all - 1)

    raw = [move(embeddings, *by) for by in RAW_MOVES]
    raw_far = move(embeddings, 0, 2)

    stats_here = pl.pallas_call(
        stats_kernel,
        out_shape=jax.ShapeDtypeStruct((rows_count, 2, col_width), F32),
        in_specs=whole(1),
        out_specs=whole(1)[0],
        name="stats",
    )(embeddings)
    stats = lax.all_to_all(stats_here, ROWS, 0, 0)
    stats, raw, minus = lax.optimization_barrier((stats, raw, -embeddings))
    sums, squares = stats[:, 0], stats[:, 1]
    mean = jnp.sum(sums, axis=0) / n_all
    gaps = sums / rows_here - mean
    var = (jnp.sum(squares, axis=0) + rows_here * jnp.sum(gaps * gaps, axis=0)) / scale
    std = jnp.sqrt(var + 0.0001)

    cz = -(minus + mean)
    along_zl, along_x = (
        jnp.concatenate([block.astype(BF16) for block in pair])
        for pair in ((cz, raw[0] - mean), (raw[1] - mean, raw[2] - mean))
    )
    centered = along_zl[:rows_here]
    far = [(raw_far - mean).astype(BF16), move(along_zl[rows_here:], 0, 2)]
    gathered = jnp.concatenate([along_zl, along_x, move(along_x, 1, 0)] + far)

    half = rows_here // 2
    piece = half // ys

    def half_gram(which):
        own = lax.dynamic_slice_in_dim(centered, which * half, half, 0)
        own = lax.dynamic_slice_in_dim(jnp.concatenate([own, own]), y * piece, half, 0)
        return lax.dot_general(
            own, gathered, (((1,), (1,)), ((), ())), preferred_element_type=F32
        )

    from_pair = lax.ppermute(half_gram(1 - core), "core", SWAP)
    from_pair, here = lax.optimization_barrier((from_pair, half_gram(core)))
    chip_half = here + from_pair
    chunks = [chip_half[k * piece : (k + 1) * piece] for k in range(ys)]
    over_y = chunks[0] + sum(shift(chunks[k], "y", k) for k in (2, 1, 3))

    gathered_f32 = gathered.astype(F32)
    col_norms = jnp.sum(gathered_f32 * gathered_f32, axis=0)
    block_share = (
        25.0 * lanes(jax.nn.relu(1.0 - std)) - lanes(col_norms * col_norms) / (scale * scale)
    ) / (width * rows_count)
    over_y = jnp.concatenate([over_y, jnp.broadcast_to(block_share, (piece, 128))], axis=1)
    mine = over_y + sum(shift(over_y, "zh", k) for k in (2, 1, 3))
    back = {k: shift(mine, "y", k) for k in (2, 1, 3)}
    blocks = [mine, back[2], back[1], back[3]]
    my_half = jnp.concatenate([block[:, :n_all] for block in blocks])
    other_half = lax.ppermute(my_half, "core", SWAP)
    blocks_share = sum(block[0, n_all:] for block in blocks)
    share = lanes(my_half * my_half) / (scale * scale * width) + blocks_share
    shares = spread(jnp.broadcast_to(share, (8, 128)), ROWS + ("core",), rows_count * 2)

    gram = jnp.zeros((rows_here, n_all), F32)
    for k, away in enumerate((0, 2, 1, 3)):
        owner = lax.rem(y + ys - away, ys)
        for c, rows in enumerate((my_half, other_half)):
            block = rows[k * piece : (k + 1) * piece]
            start = lax.rem(core + c, 2) * half + owner * piece
            gram = lax.dynamic_update_slice_in_dim(gram, block, start, 0)
    terms = jnp.dot(three_terms(gram), gathered, preferred_element_type=F32)
    product = terms[:rows_here] + terms[rows_here : 2 * rows_here] + terms[2 * rows_here :]
    grad_cov = (product - centered.astype(F32) * col_norms) / scale
    hinge = jnp.where(std < 1.0, cz / std, F32(0.0))
    grad_scaled = 4.0 / 25.0 * grad_cov - hinge
    grad_scaled, shares = lax.optimization_barrier((grad_scaled, shares))
    return (grad_scaled, jnp.sum(shares[:, 0]))


def solution(mesh):
    parts = Mesh(mesh.devices.reshape(2, 4, 4, 4, 2), ("zl", "x", "y", "zh", "core"))
    placed = P(("zl", "x"), ("y", "zh", "core"))
    return jax.shard_map(
        on_device, mesh=parts, in_specs=(placed,), out_specs=(placed, P()), check_vma=False
    )
```

```python
import functools

import jax
import jax.numpy as jnp
from jax import lax
from jax.experimental import pallas as pl
from jax.experimental.pallas import tpu as pltpu
from jax.sharding import Mesh
from jax.sharding import PartitionSpec as P

ROWS = ("zl", "x")
SWAP = [(0, 1), (1, 0)]
F32 = jnp.float32
BF16 = jnp.bfloat16


def spread(block, axes, count):
    return lax.all_to_all(jnp.broadcast_to(block, (count,) + block.shape), axes, 0, 0)


def shift(block, axis, k):
    size = lax.axis_size(axis)
    return lax.ppermute(block, axis, [(i, (i + k) % size) for i in range(size)])


RAW_MOVES = ((1, 0), (0, 1), (0, 3))


def move(block, along_zl, along_x):
    zls, xs = lax.axis_size("zl"), lax.axis_size("x")
    return lax.ppermute(
        block,
        ROWS,
        [
            (z * xs + x, (z + along_zl) % zls * xs + (x + along_x) % xs)
            for z in range(zls)
            for x in range(xs)
        ],
    )


def stats_kernel(block_ref, out_ref):
    block = block_ref[...]
    total = jnp.sum(block, axis=0, keepdims=True)
    off = block - total / block.shape[0]
    squares = jnp.sum(off * off, axis=0, keepdims=True)
    both = jnp.concatenate([total, squares], axis=0)
    for k in range(out_ref.shape[0]):
        out_ref[k] = both


def share_kernel(n_all, factor, *refs):
    blocks, out_ref = refs[:-1], refs[-1]
    rows = blocks[0].shape[0]
    squares = jnp.zeros((rows, 128), F32)
    beside = jnp.zeros((1, 128), F32)
    for block_ref in blocks:
        for first in range(0, n_all, 128):
            part = block_ref[:, first : first + 128]
            squares += part * part
        beside += block_ref[:1, n_all:]
    share = jnp.sum(squares, axis=0, keepdims=True) * factor + beside
    for k in range(out_ref.shape[0]):
        out_ref[k] = jnp.broadcast_to(share, (8, 128))


def whole(count):
    return [pl.BlockSpec(memory_space=pltpu.VMEM)] * count


def three_terms(a):
    high = lax.reduce_precision(a, 8, 7)
    rest = a - high
    mid = lax.reduce_precision(rest, 8, 7)
    low = rest - mid
    return jnp.concatenate([high.astype(BF16), mid.astype(BF16), low.astype(BF16)], axis=0)


def lanes(a):
    return jnp.sum(a.reshape(-1, 128), axis=0)


def on_device(embeddings):
    rows_here, col_width = embeddings.shape
    rows_count = lax.axis_size(ROWS)
    ys = lax.axis_size("y")
    cols_count = ys * lax.axis_size("zh") * lax.axis_size("core")
    core = lax.axis_index("core")
    y = lax.axis_index("y")
    n_all = rows_here * rows_count
    width = col_width * cols_count
    scale = F32(n_all - 1)

    raw = [move(embeddings, *by) for by in RAW_MOVES]
    raw_far = move(embeddings, 0, 2)

    stats_here = pl.pallas_call(
        stats_kernel,
        out_shape=jax.ShapeDtypeStruct((rows_count, 2, col_width), F32),
        in_specs=whole(1),
        out_specs=whole(1)[0],
        name="stats",
    )(embeddings)
    stats = lax.all_to_all(stats_here, ROWS, 0, 0)
    stats, raw, minus = lax.optimization_barrier((stats, raw, -embeddings))
    sums, squares = stats[:, 0], stats[:, 1]
    mean = jnp.sum(sums, axis=0) / n_all
    gaps = sums / rows_here - mean
    var = (jnp.sum(squares, axis=0) + rows_here * jnp.sum(gaps * gaps, axis=0)) / scale
    std = jnp.sqrt(var + 0.0001)

    cz = -(minus + mean)
    along_zl, along_x = (
        jnp.concatenate([block.astype(BF16) for block in pair])
        for pair in ((cz, raw[0] - mean), (raw[1] - mean, raw[2] - mean))
    )
    centered = along_zl[:rows_here]
    far = [(raw_far - mean).astype(BF16), move(along_zl[rows_here:], 0, 2)]
    early = jnp.concatenate([along_zl, along_x])
    late = jnp.concatenate([move(along_x, 1, 0)] + far)
    gathered = jnp.concatenate([early, late])

    half = rows_here // 2
    piece = half // ys

    def half_gram(which, rows):
        own = lax.dynamic_slice_in_dim(centered, which * half, half, 0)
        own = lax.dynamic_slice_in_dim(jnp.concatenate([own, own]), y * piece, half, 0)
        return lax.dot_general(
            own, rows, (((1,), (1,)), ((), ())), preferred_element_type=F32
        )

    from_pair = [lax.ppermute(half_gram(1 - core, rows), "core", SWAP) for rows in (early, late)]
    here = [half_gram(core, rows) for rows in (early, late)]
    from_pair, here = lax.optimization_barrier((from_pair, here))
    chip_half = jnp.concatenate([a + b for a, b in zip(from_pair, here)], axis=1)
    chunks = [chip_half[k * piece : (k + 1) * piece] for k in range(ys)]
    over_y = chunks[0] + sum(shift(chunks[k], "y", k) for k in (1, 3, 2))

    halves = [rows.astype(F32) for rows in (early, late)]
    col_norms = sum(jnp.sum(rows * rows, axis=0) for rows in halves)
    block_share = (
        25.0 * lanes(jax.nn.relu(1.0 - std)) - lanes(col_norms * col_norms) / (scale * scale)
    ) / (width * rows_count)
    over_y = jnp.concatenate([over_y, jnp.broadcast_to(block_share, (piece, 128))], axis=1)
    mine = over_y + sum(shift(over_y, "zh", k) for k in (2, 1, 3))
    back = {k: shift(mine, "y", k) for k in (2, 1, 3)}
    blocks = [mine, back[2], back[1], back[3]]
    my_half = jnp.concatenate([block[:, :n_all] for block in blocks])
    other_half = lax.ppermute(my_half, "core", SWAP)
    shares_here = pl.pallas_call(
        functools.partial(share_kernel, n_all, 1.0 / (float(n_all - 1) ** 2 * width)),
        out_shape=jax.ShapeDtypeStruct((rows_count * 2, 8, 128), F32),
        in_specs=whole(ys),
        out_specs=whole(1)[0],
        name="share",
    )(*(pltpu.with_memory_space_constraint(block, pltpu.VMEM) for block in blocks))
    shares = lax.all_to_all(shares_here, ROWS + ("core",), 0, 0)

    product = jnp.zeros((rows_here, col_width), F32)
    for c, rows in enumerate((my_half, other_half)):
        gram = jnp.zeros((half, n_all), F32)
        for k, away in enumerate((0, 2, 1, 3)):
            owner = lax.rem(y + ys - away, ys)
            gram = lax.dynamic_update_slice_in_dim(
                gram, rows[k * piece : (k + 1) * piece], owner * piece, 0
            )
        terms = jnp.dot(three_terms(gram), gathered, preferred_element_type=F32)
        part = terms[:half] + terms[half : 2 * half] + terms[2 * half :]
        start = lax.rem(core + c, 2) * half
        product = lax.dynamic_update_slice_in_dim(product, part, start, 0)
    grad_cov = (product - centered.astype(F32) * col_norms) / scale
    hinge = jnp.where(std < 1.0, cz / std, F32(0.0))
    grad_scaled = 4.0 / 25.0 * grad_cov - hinge
    grad_scaled, shares = lax.optimization_barrier((grad_scaled, shares))
    return (grad_scaled, jnp.sum(shares[:, 0]))


def solution(mesh):
    parts = Mesh(mesh.devices.reshape(2, 4, 4, 4, 2), ("zl", "x", "y", "zh", "core"))
    placed = P(("zl", "x"), ("y", "zh", "core"))
    return jax.shard_map(
        on_device, mesh=parts, in_specs=(placed,), out_specs=(placed, P()), check_vma=False
    )
```

```python
import functools

import jax
import jax.numpy as jnp
from jax import lax
from jax.experimental import pallas as pl
from jax.experimental.pallas import tpu as pltpu
from jax.sharding import Mesh
from jax.sharding import PartitionSpec as P

ROWS = ("zl", "x")
SWAP = [(0, 1), (1, 0)]
F32 = jnp.float32
BF16 = jnp.bfloat16


def spread(block, axes, count):
    return lax.all_to_all(jnp.broadcast_to(block, (count,) + block.shape), axes, 0, 0)


def shift(block, axis, k):
    size = lax.axis_size(axis)
    return lax.ppermute(block, axis, [(i, (i + k) % size) for i in range(size)])


RAW_MOVES = ((1, 0), (0, 1), (0, 3))


def move(block, along_zl, along_x):
    zls, xs = lax.axis_size("zl"), lax.axis_size("x")
    return lax.ppermute(
        block,
        ROWS,
        [
            (z * xs + x, (z + along_zl) % zls * xs + (x + along_x) % xs)
            for z in range(zls)
            for x in range(xs)
        ],
    )


def stats_kernel(block_ref, out_ref):
    block = block_ref[...]
    total = jnp.sum(block, axis=0, keepdims=True)
    off = block - total / block.shape[0]
    squares = jnp.sum(off * off, axis=0, keepdims=True)
    both = jnp.concatenate([total, squares], axis=0)
    for k in range(out_ref.shape[0]):
        out_ref[k] = both


def share_kernel(n_all, factor, *refs):
    blocks, out_ref = refs[:-1], refs[-1]
    rows = blocks[0].shape[0]
    squares = jnp.zeros((rows, 128), F32)
    beside = jnp.zeros((1, 128), F32)
    for block_ref in blocks:
        for first in range(0, n_all, 128):
            part = block_ref[:, first : first + 128]
            squares += part * part
        beside += block_ref[:1, n_all:]
    share = jnp.sum(squares, axis=0, keepdims=True) * factor + beside
    for k in range(out_ref.shape[0]):
        out_ref[k] = jnp.broadcast_to(share, (8, 128))


def whole(count):
    return [pl.BlockSpec(memory_space=pltpu.VMEM)] * count


def three_terms(a):
    high = lax.reduce_precision(a, 8, 7)
    rest = a - high
    mid = lax.reduce_precision(rest, 8, 7)
    low = rest - mid
    return jnp.concatenate([high.astype(BF16), mid.astype(BF16), low.astype(BF16)], axis=0)


def lanes(a):
    return jnp.sum(a.reshape(-1, 128), axis=0)


def on_device(embeddings):
    rows_here, col_width = embeddings.shape
    rows_count = lax.axis_size(ROWS)
    ys = lax.axis_size("y")
    cols_count = ys * lax.axis_size("zh") * lax.axis_size("core")
    core = lax.axis_index("core")
    y = lax.axis_index("y")
    n_all = rows_here * rows_count
    width = col_width * cols_count
    scale = F32(n_all - 1)

    stats_here = pl.pallas_call(
        stats_kernel,
        out_shape=jax.ShapeDtypeStruct((rows_count, 2, col_width), F32),
        in_specs=whole(1),
        out_specs=whole(1)[0],
        name="stats",
    )(embeddings)
    stats_here, sent = lax.optimization_barrier((stats_here, embeddings))
    raw = [move(sent, *by) for by in RAW_MOVES]
    raw_far = move(sent, 0, 2)
    stats = lax.all_to_all(stats_here, ROWS, 0, 0)
    stats, raw, minus = lax.optimization_barrier((stats, raw, -embeddings))
    sums, squares = stats[:, 0], stats[:, 1]
    mean = jnp.sum(sums, axis=0) / n_all
    gaps = sums / rows_here - mean
    var = (jnp.sum(squares, axis=0) + rows_here * jnp.sum(gaps * gaps, axis=0)) / scale
    std = jnp.sqrt(var + 0.0001)

    cz = -(minus + mean)
    along_zl, along_x = (
        jnp.concatenate([block.astype(BF16) for block in pair])
        for pair in ((cz, raw[0] - mean), (raw[1] - mean, raw[2] - mean))
    )
    centered = along_zl[:rows_here]
    far = [(raw_far - mean).astype(BF16), move(along_zl[rows_here:], 0, 2)]
    early = jnp.concatenate([along_zl, along_x])
    late = jnp.concatenate([move(along_x, 1, 0)] + far)
    gathered = jnp.concatenate([early, late])

    half = rows_here // 2
    piece = half // ys

    def half_gram(which, rows):
        own = lax.dynamic_slice_in_dim(centered, which * half, half, 0)
        own = lax.dynamic_slice_in_dim(jnp.concatenate([own, own]), y * piece, half, 0)
        return lax.dot_general(
            own, rows, (((1,), (1,)), ((), ())), preferred_element_type=F32
        )

    from_pair = [lax.ppermute(half_gram(1 - core, rows), "core", SWAP) for rows in (early, late)]
    here = [half_gram(core, rows) for rows in (early, late)]
    from_pair, here = lax.optimization_barrier((from_pair, here))
    chip_half = jnp.concatenate([a + b for a, b in zip(from_pair, here)], axis=1)
    chunks = [chip_half[k * piece : (k + 1) * piece] for k in range(ys)]
    over_y = chunks[0] + sum(shift(chunks[k], "y", k) for k in (1, 3, 2))

    halves = [rows.astype(F32) for rows in (early, late)]
    col_norms = sum(jnp.sum(rows * rows, axis=0) for rows in halves)
    block_share = (
        25.0 * lanes(jax.nn.relu(1.0 - std)) - lanes(col_norms * col_norms) / (scale * scale)
    ) / (width * rows_count)
    over_y = jnp.concatenate([over_y, jnp.broadcast_to(block_share, (piece, 128))], axis=1)
    mine = over_y + sum(shift(over_y, "zh", k) for k in (2, 1, 3))
    back = {k: shift(mine, "y", k) for k in (2, 1, 3)}
    blocks = [mine, back[2], back[1], back[3]]
    my_half = jnp.concatenate([block[:, :n_all] for block in blocks])
    other_half = lax.ppermute(my_half, "core", SWAP)
    shares_here = pl.pallas_call(
        functools.partial(share_kernel, n_all, 1.0 / (float(n_all - 1) ** 2 * width)),
        out_shape=jax.ShapeDtypeStruct((rows_count * 2, 8, 128), F32),
        in_specs=whole(ys),
        out_specs=whole(1)[0],
        name="share",
    )(*(pltpu.with_memory_space_constraint(block, pltpu.VMEM) for block in blocks))
    shares = lax.all_to_all(shares_here, ROWS + ("core",), 0, 0)

    product = jnp.zeros((rows_here, col_width), F32)
    for c, rows in enumerate((my_half, other_half)):
        gram = jnp.zeros((half, n_all), F32)
        for k, away in enumerate((0, 2, 1, 3)):
            owner = lax.rem(y + ys - away, ys)
            gram = lax.dynamic_update_slice_in_dim(
                gram, rows[k * piece : (k + 1) * piece], owner * piece, 0
            )
        terms = jnp.dot(three_terms(gram), gathered, preferred_element_type=F32)
        part = terms[:half] + terms[half : 2 * half] + terms[2 * half :]
        start = lax.rem(core + c, 2) * half
        product = lax.dynamic_update_slice_in_dim(product, part, start, 0)
    grad_cov = (product - centered.astype(F32) * col_norms) / scale
    hinge = jnp.where(std < 1.0, cz / std, F32(0.0))
    grad_scaled = 4.0 / 25.0 * grad_cov - hinge
    grad_scaled, shares = lax.optimization_barrier((grad_scaled, shares))
    return (grad_scaled, jnp.sum(shares[:, 0]))


def solution(mesh):
    parts = Mesh(mesh.devices.reshape(2, 4, 4, 4, 2), ("zl", "x", "y", "zh", "core"))
    placed = P(("zl", "x"), ("y", "zh", "core"))
    return jax.shard_map(
        on_device, mesh=parts, in_specs=(placed,), out_specs=(placed, P()), check_vma=False
    )
```

```python
import functools

import jax
import jax.numpy as jnp
from jax import lax
from jax.experimental import pallas as pl
from jax.experimental.pallas import tpu as pltpu
from jax.sharding import Mesh
from jax.sharding import PartitionSpec as P

ROWS = ("zl", "x")
SWAP = [(0, 1), (1, 0)]
F32 = jnp.float32
BF16 = jnp.bfloat16


def spread(block, axes, count):
    return lax.all_to_all(jnp.broadcast_to(block, (count,) + block.shape), axes, 0, 0)


def shift(block, axis, k):
    size = lax.axis_size(axis)
    return lax.ppermute(block, axis, [(i, (i + k) % size) for i in range(size)])


RAW_MOVES = ((1, 0), (0, 1), (0, 3))


def move(block, along_zl, along_x):
    zls, xs = lax.axis_size("zl"), lax.axis_size("x")
    return lax.ppermute(
        block,
        ROWS,
        [
            (z * xs + x, (z + along_zl) % zls * xs + (x + along_x) % xs)
            for z in range(zls)
            for x in range(xs)
        ],
    )


def stats_kernel(source_ref, out_ref, block_ref, sems):
    pieces = sems.shape[0]
    rows = block_ref.shape[0] // pieces
    copies = [
        pltpu.make_async_copy(
            source_ref.at[k * rows : (k + 1) * rows],
            block_ref.at[k * rows : (k + 1) * rows],
            sems.at[k],
        )
        for k in range(pieces)
    ]
    for copy in copies:
        copy.start()
    partial = jnp.zeros((rows, block_ref.shape[1]), F32)
    for k, copy in enumerate(copies):
        copy.wait()
        partial += block_ref[k * rows : (k + 1) * rows]
    total = jnp.sum(partial, axis=0, keepdims=True)
    off = block_ref[...] - total / block_ref.shape[0]
    squares = jnp.sum(off * off, axis=0, keepdims=True)
    both = jnp.concatenate([total, squares], axis=0)
    for k in range(out_ref.shape[0]):
        out_ref[k] = both


def share_kernel(n_all, factor, *refs):
    blocks, out_ref = refs[:-1], refs[-1]
    rows = blocks[0].shape[0]
    squares = jnp.zeros((rows, 128), F32)
    beside = jnp.zeros((1, 128), F32)
    for block_ref in blocks:
        for first in range(0, n_all, 128):
            part = block_ref[:, first : first + 128]
            squares += part * part
        beside += block_ref[:1, n_all:]
    share = jnp.sum(squares, axis=0, keepdims=True) * factor + beside
    for k in range(out_ref.shape[0]):
        out_ref[k] = jnp.broadcast_to(share, (2, 128))


def whole(count):
    return [pl.BlockSpec(memory_space=pltpu.VMEM)] * count


def three_terms(a):
    high = lax.reduce_precision(a, 8, 7)
    rest = a - high
    mid = lax.reduce_precision(rest, 8, 7)
    low = rest - mid
    return jnp.concatenate([high.astype(BF16), mid.astype(BF16), low.astype(BF16)], axis=0)


def lanes(a):
    return jnp.sum(a.reshape(-1, 128), axis=0)


def on_device(embeddings):
    rows_here, col_width = embeddings.shape
    rows_count = lax.axis_size(ROWS)
    ys = lax.axis_size("y")
    cols_count = ys * lax.axis_size("zh") * lax.axis_size("core")
    core = lax.axis_index("core")
    y = lax.axis_index("y")
    n_all = rows_here * rows_count
    width = col_width * cols_count
    scale = F32(n_all - 1)

    raw = [move(embeddings, *by) for by in RAW_MOVES]
    raw_far = move(embeddings, 0, 2)

    stats_here = pl.pallas_call(
        stats_kernel,
        out_shape=jax.ShapeDtypeStruct((rows_count, 2, col_width), F32),
        in_specs=[pl.BlockSpec(memory_space=pltpu.HBM)],
        out_specs=whole(1)[0],
        scratch_shapes=[
            pltpu.VMEM((rows_here, col_width), F32),
            pltpu.SemaphoreType.DMA((8,)),
        ],
        name="stats",
    )(embeddings)
    stats = lax.all_to_all(stats_here, ROWS, 0, 0)
    stats, raw, minus = lax.optimization_barrier((stats, raw, -embeddings))
    sums, squares = stats[:, 0], stats[:, 1]
    mean = jnp.sum(sums, axis=0) / n_all
    gaps = sums / rows_here - mean
    var = (jnp.sum(squares, axis=0) + rows_here * jnp.sum(gaps * gaps, axis=0)) / scale
    std = jnp.sqrt(var + 0.0001)

    cz = -(minus + mean)
    along_zl, along_x = (
        jnp.concatenate([block.astype(BF16) for block in pair])
        for pair in ((cz, raw[0] - mean), (raw[1] - mean, raw[2] - mean))
    )
    centered = along_zl[:rows_here]
    far = [(raw_far - mean).astype(BF16), move(along_zl[rows_here:], 0, 2)]
    early = jnp.concatenate([along_zl, along_x])
    late = jnp.concatenate([move(along_x, 1, 0)] + far)
    gathered = jnp.concatenate([early, late])

    half = rows_here // 2
    piece = half // ys

    def half_gram(which, rows):
        own = lax.dynamic_slice_in_dim(centered, which * half, half, 0)
        own = lax.dynamic_slice_in_dim(jnp.concatenate([own, own]), y * piece, half, 0)
        return lax.dot_general(
            own, rows, (((1,), (1,)), ((), ())), preferred_element_type=F32
        )

    from_pair = [lax.ppermute(half_gram(1 - core, rows), "core", SWAP) for rows in (early, late)]
    here = [half_gram(core, rows) for rows in (early, late)]
    from_pair, here = lax.optimization_barrier((from_pair, here))
    chip_half = jnp.concatenate([a + b for a, b in zip(from_pair, here)], axis=1)
    chunks = [chip_half[k * piece : (k + 1) * piece] for k in range(ys)]
    over_y = chunks[0] + sum(shift(chunks[k], "y", k) for k in (1, 3, 2))

    halves = [rows.astype(F32) for rows in (early, late)]
    col_norms = sum(jnp.sum(rows * rows, axis=0) for rows in halves)
    block_share = (
        25.0 * lanes(jax.nn.relu(1.0 - std)) - lanes(col_norms * col_norms) / (scale * scale)
    ) / (width * rows_count)
    over_y = jnp.concatenate([over_y, jnp.broadcast_to(block_share, (piece, 128))], axis=1)
    mine = over_y + sum(shift(over_y, "zh", k) for k in (2, 1, 3))
    back = {k: shift(mine, "y", k) for k in (2, 1, 3)}
    blocks = [mine, back[2], back[1], back[3]]
    my_half = jnp.concatenate([block[:, :n_all] for block in blocks])
    other_half = lax.ppermute(my_half, "core", SWAP)
    shares_here = pl.pallas_call(
        functools.partial(share_kernel, n_all, 1.0 / (float(n_all - 1) ** 2 * width)),
        out_shape=jax.ShapeDtypeStruct((rows_count * 2, 2, 128), F32),
        in_specs=whole(ys),
        out_specs=whole(1)[0],
        name="share",
    )(*(pltpu.with_memory_space_constraint(block, pltpu.VMEM) for block in blocks))
    shares = lax.all_to_all(shares_here, ROWS + ("core",), 0, 0)

    product = jnp.zeros((rows_here, col_width), F32)
    for c, rows in enumerate((my_half, other_half)):
        gram = jnp.zeros((half, n_all), F32)
        for k, away in enumerate((0, 2, 1, 3)):
            owner = lax.rem(y + ys - away, ys)
            gram = lax.dynamic_update_slice_in_dim(
                gram, rows[k * piece : (k + 1) * piece], owner * piece, 0
            )
        terms = jnp.dot(three_terms(gram), gathered, preferred_element_type=F32)
        part = terms[:half] + terms[half : 2 * half] + terms[2 * half :]
        start = lax.rem(core + c, 2) * half
        product = lax.dynamic_update_slice_in_dim(product, part, start, 0)
    grad_cov = (product - centered.astype(F32) * col_norms) / scale
    hinge = jnp.where(std < 1.0, cz / std, F32(0.0))
    grad_scaled = 4.0 / 25.0 * grad_cov - hinge
    grad_scaled, shares = lax.optimization_barrier((grad_scaled, shares))
    return (grad_scaled, jnp.sum(shares[:, 0]))


def solution(mesh):
    parts = Mesh(mesh.devices.reshape(2, 4, 4, 4, 2), ("zl", "x", "y", "zh", "core"))
    placed = P(("zl", "x"), ("y", "zh", "core"))
    return jax.shard_map(
        on_device, mesh=parts, in_specs=(placed,), out_specs=(placed, P()), check_vma=False
    )
```
